32 devices in a mesh: dp: 16 (over z, y, core), tensor: 2 (over x).
Axes of the slice: x: 2, y: 2, z: 4, core: 2. Of those that a mesh axis runs over, the one named last changes fastest.
Arguments:
- tokens: bfloat16 [16384, 1024], P(('dp', 'tensor')), may hold values from -6 to 6
- lengths: int32 [16, 4], P('dp'), may hold values from 0 to 1024, as said below
- attn_gain: bfloat16 [1024], P('dp'), may hold values from 0.5 to 1.5
- w_query: bfloat16 [1024, 1024], P('dp', 'tensor'), may hold values from -0.1875 to 0.1875
- key_weight: bfloat16 [1024, 512], P('dp', 'tensor'), may hold values from -0.1875 to 0.1875
- value_weight: bfloat16 [1024, 512], P('dp', 'tensor'), may hold values from -0.1875 to 0.1875
- query_gain: bfloat16 [64], replicated, may hold values from 0.5 to 1.5
- key_gain: bfloat16 [64], replicated, may hold values from 0.5 to 1.5
- w_out: bfloat16 [1024, 1024], P('tensor', 'dp'), may hold values from -3 to 3
- ffn_gain: bfloat16 [1024], P('dp'), may hold values from 0.5 to 1.5
- w_gate: bfloat16 [1024, 4608], P('dp', 'tensor'), may hold values from -0.1875 to 0.1875
- w_up: bfloat16 [1024, 4608], P('dp', 'tensor'), may hold values from -0.1875 to 0.1875
- w_down: bfloat16 [4608, 1024], P('tensor', 'dp'), may hold values from -0.09375 to 0.09375
- out_grad: bfloat16 [16384, 1024], P(('dp', 'tensor')), may hold values from -6 to 6
Outputs:
- output: bfloat16 [16384, 1024], P(('dp', 'tensor'))
- input_grad: float32 [16384, 1024], P(('dp', 'tensor'))
- attn_gain_grad: float32 [1024], P('dp')
- w_query_grad: float32 [1024, 1024], P('dp', 'tensor')
- w_key_grad: float32 [1024, 512], P('dp', 'tensor')
- w_value_grad: float32 [1024, 512], P('dp', 'tensor')
- query_gain_grad: float32 [64], replicated
- key_gain_grad: float32 [64], replicated
- w_out_grad: float32 [1024, 1024], P('tensor', 'dp')
- ffn_gain_grad: float32 [1024], P('dp')
- w_gate_grad: float32 [1024, 4608], P('dp', 'tensor')
- w_up_grad: float32 [1024, 4608], P('dp', 'tensor')
- w_down_grad: float32 [4608, 1024], P('tensor', 'dp')
The draws below stay inside these ranges and needn't reach their ends.
Inputs may be any that keep to these rules, and one draw needn't show every extreme that they name: Each row lists the lengths of one group's sequences in slot order, packed from the group's first slot; a row sums to at most 1024 and the slots after the last sequence are padding.
All inputs are finite; a program needn't handle non-finite values.
Results may differ from the reference program's by a relative error of at most 0.018.
Values may be sent and summed in bfloat16 or wider, within the bound.
A program may use at most 256 MiB of HBM per device.

```python
from functools import partial
import jax
import jax.numpy as jnp
from jax import lax

MODEL_WIDTH = 1024
FF = 4608
QUERY_HEADS = 16
KEY_VALUE_HEADS = 8
HEAD_SIZE = 64
GROUP_LENGTH = 1024
SEQS = 4
TOK_DEV = 512
TOKEN_SLOTS = 16384
N_DP = 16


def draw_lengths(key, part):
    key = jax.random.fold_in(key, 17)
    key_spare, key_chosen, key_cuts, key_slot = jax.random.split(key, 4)
    spare_slots = jax.random.randint(key_spare, (N_DP,), 0, TOK_DEV)
    chosen = jax.random.randint(key_chosen, (), 0, N_DP)
    spare_slots = jnp.where(jnp.arange(N_DP) == chosen, 0, spare_slots)
    long_length = GROUP_LENGTH - spare_slots
    cut_points = jax.random.randint(key_cuts, (N_DP, SEQS - 1), 0, TOK_DEV) % (spare_slots[:, None] + 1)
    cut_points = jnp.sort(cut_points, axis=1)
    shorts = jnp.diff(jnp.concatenate([jnp.zeros((N_DP, 1), jnp.int32), cut_points.astype(jnp.int32)], axis=1), axis=1)
    long_slot = jax.random.randint(key_slot, (N_DP, 1), 0, SEQS)
    places = jnp.arange(SEQS)[None, :]
    short_index = jnp.clip(jnp.where(places < long_slot, places, places - 1), 0, SEQS - 2)
    shorts_at = jnp.take_along_axis(shorts, jnp.broadcast_to(short_index, (N_DP, SEQS)), axis=1)
    return jnp.where(places == long_slot, long_length[:, None], shorts_at).astype(jnp.int32)


def level_of(rng, extent, cuts, low, largest):
    gain = 1.0
    for dim, parts in cuts:
        steps = jax.random.uniform(jax.random.fold_in(jax.random.fold_in(rng, 6), dim), (parts,), jnp.float32, low / len(cuts), largest / len(cuts))
        gain = gain * jnp.repeat(jnp.exp(steps), extent[dim] // parts).reshape((-1,) + (1,) * (len(extent) - 1 - dim))
    return gain


def scatter_about(rng, extent, deviation, reach, cuts=(), kind=jnp.bfloat16):
    drawn = jax.random.normal(rng, extent, jnp.float32) * deviation
    if len(cuts) > 0:
        drawn = level_of(rng, extent, cuts, -0.22, 0.18) * drawn
    return jnp.clip(drawn, min=-reach, max=reach).astype(kind)


def setup_inputs(seed: int = 0) -> dict:
    streams_of = jax.random.split(jax.random.key(seed), 15)
    return {
        "tokens": scatter_about(streams_of[0], (TOKEN_SLOTS, MODEL_WIDTH), 1.0, 6.0, ((0, 32),)),
        "lengths": draw_lengths(jax.random.fold_in(streams_of[14], 71), 0),
        "attn_gain": jnp.clip(1.0 + 0.1 * jax.random.normal(streams_of[2], (MODEL_WIDTH,), jnp.float32), 0.5, 1.5).astype(jnp.bfloat16),
        "w_query": scatter_about(streams_of[3], (MODEL_WIDTH, QUERY_HEADS * HEAD_SIZE), MODEL_WIDTH ** -0.5, 0.1875, ((0, 16), (1, 2))),
        "key_weight": scatter_about(streams_of[4], (MODEL_WIDTH, KEY_VALUE_HEADS * HEAD_SIZE), MODEL_WIDTH ** -0.5, 0.1875, ((0, 16), (1, 2))),
        "value_weight": scatter_about(streams_of[5], (MODEL_WIDTH, KEY_VALUE_HEADS * HEAD_SIZE), MODEL_WIDTH ** -0.5, 0.1875, ((0, 16), (1, 2))),
        "query_gain": jnp.clip(1.0 + 0.1 * jax.random.normal(streams_of[6], (HEAD_SIZE,), jnp.float32), 0.5, 1.5).astype(jnp.bfloat16),
        "key_gain": jnp.clip(1.0 + 0.1 * jax.random.normal(streams_of[7], (HEAD_SIZE,), jnp.float32), 0.5, 1.5).astype(jnp.bfloat16),
        "w_out": scatter_about(streams_of[8], (QUERY_HEADS * HEAD_SIZE, MODEL_WIDTH), (4 * QUERY_HEADS * HEAD_SIZE // GROUP_LENGTH) ** -0.5, 3.0, ((0, 2), (1, 16))),
        "ffn_gain": jnp.clip(1.0 + 0.1 * jax.random.normal(streams_of[9], (MODEL_WIDTH,), jnp.float32), 0.5, 1.5).astype(jnp.bfloat16),
        "w_gate": scatter_about(streams_of[10], (MODEL_WIDTH, FF), MODEL_WIDTH ** -0.5, 0.1875, ((0, 16), (1, 2))),
        "w_up": scatter_about(streams_of[11], (MODEL_WIDTH, FF), MODEL_WIDTH ** -0.5, 0.1875, ((0, 16), (1, 2))),
        "w_down": scatter_about(streams_of[12], (FF, MODEL_WIDTH), FF ** -0.5, 0.09375, ((0, 2), (1, 16))),
        "out_grad": scatter_about(streams_of[13], (TOKEN_SLOTS, MODEL_WIDTH), 1.0, 6.0, ((0, 32),)),
    }


EPSILON = 1e-05
ROPE_BASE = 1000000.0
MASK_FILL = -1e+30
PRECISE = lax.Precision.HIGHEST

@jax.custom_vjp
def lower_precision(v):
    return lax.optimization_barrier(v.astype(jnp.bfloat16)).astype(jnp.float32)

@jax.custom_vjp
def low_back(v):
    return v

def low_keep(v):
    return (lower_precision(v), None)

def low_pass(kept, grad):
    return (grad,)

def back_keep(v):
    return (v, None)

def back_low(kept, grad):
    return (lower_precision(grad),)
lower_precision.defvjp(low_keep, low_pass)
low_back.defvjp(back_keep, back_low)

def segments(seq_lengths, total_slots):
    ends = jnp.cumsum(seq_lengths).astype(jnp.int32)
    starts = (ends - seq_lengths).astype(jnp.int32)
    places = jnp.arange(total_slots, dtype=jnp.int32)
    segment_index = lax.optimization_barrier(jnp.sum((places[:, None] >= ends[None, :]).astype(jnp.int32), axis=1)).astype(jnp.int32)
    number = seq_lengths.shape[0]
    chosen = segment_index[:, None] == jnp.arange(number, dtype=jnp.int32)[None, :]
    first_slot = lax.optimization_barrier(jnp.sum(jnp.where(chosen, starts[None, :], 0), axis=1)).astype(jnp.int32)
    return (segment_index, places - first_slot, segment_index < number)

def block_mask(segment_index, valid_mask, low_row, high_row, key_count):
    query_places = jnp.arange(low_row, high_row)
    key_places = jnp.arange(key_count)
    causal = key_places[None, :] <= query_places[:, None]
    same = (segment_index[low_row:high_row, None] == segment_index[None, :key_count]) & valid_mask[low_row:high_row, None] & causal
    return same | (key_places[None, :] == query_places[:, None])

def rows_normalize(values, gain_vec):
    return values * lax.rsqrt(lax.optimization_barrier(jnp.mean(values * values, axis=-1, keepdims=True)) + EPSILON) * gain_vec

def rope_tables(position, width):
    half_width = width // 2
    frequency = ROPE_BASE ** (-(jnp.arange(half_width).astype(jnp.float32) * 2.0 / width))
    angles = position.astype(jnp.float32)[:, None] * frequency[None, :]
    return (jnp.cos(angles)[:, None, :], jnp.sin(angles)[:, None, :])

def apply_rotary(values, cosine_table, sine_table):
    half_width = values.shape[-1] // 2
    first_half = values[..., :half_width]
    second_half = values[..., half_width:]
    return jnp.concatenate([first_half * cosine_table - second_half * sine_table, second_half * cosine_table + first_half * sine_table], axis=-1)

def attend_heads(inputs):
    query_rows, keys_in, values_in, segment_index, valid_mask = inputs
    slot_count = query_rows.shape[0]
    kv_count = keys_in.shape[1]
    width = query_rows.shape[-1]
    grouped = query_rows.reshape(slot_count, kv_count, -1, width)
    scores = jnp.einsum('qgrd,kgd->grqk', grouped, keys_in, precision=PRECISE, preferred_element_type=jnp.float32)
    scores = low_back(scores * width ** (-0.5))
    allowed = block_mask(segment_index, valid_mask, 0, slot_count, slot_count)
    scores = jnp.where(allowed[None, None], scores, MASK_FILL)
    row_peak = lax.optimization_barrier(jnp.max(scores, axis=-1, keepdims=True))
    exp_terms = jnp.exp(scores - row_peak)
    probs = lower_precision(exp_terms / lax.optimization_barrier(jnp.sum(exp_terms, axis=-1, keepdims=True)))
    mixed = jnp.einsum('grqk,kgd->qgrd', probs, values_in, precision=PRECISE, preferred_element_type=jnp.float32)
    return low_back(lower_precision(mixed.reshape(slot_count, -1)))

def matmul(left, right):
    return jnp.dot(left, right, precision=PRECISE, preferred_element_type=jnp.float32)

def forward(tokens_f, attn_gain_f, w_query_f, w_key_f, w_value_f, query_gain_f, key_gain_float, w_out_f, ffn_gain_f, w_gate_f, w_up_f, w_down_f, segment_index=None, position=None, valid_mask=None):
    attn_in = lower_precision(rows_normalize(tokens_f, attn_gain_f))
    query_raw = low_back(matmul(attn_in, w_query_f))
    key_unrotated = low_back(matmul(attn_in, w_key_f))
    value_lowered = lower_precision(low_back(matmul(attn_in, w_value_f)))
    cosine_table, sine_table = rope_tables(position.reshape(-1), HEAD_SIZE)
    query_rows = lower_precision(apply_rotary(rows_normalize(query_raw.reshape(TOKEN_SLOTS, QUERY_HEADS, HEAD_SIZE), query_gain_f), cosine_table, sine_table))
    key_rows_full = lower_precision(apply_rotary(rows_normalize(key_unrotated.reshape(TOKEN_SLOTS, KEY_VALUE_HEADS, HEAD_SIZE), key_gain_float), cosine_table, sine_table))
    head_outputs = lax.map(jax.checkpoint(attend_heads), (query_rows.reshape(N_DP, GROUP_LENGTH, QUERY_HEADS, HEAD_SIZE), key_rows_full.reshape(N_DP, GROUP_LENGTH, KEY_VALUE_HEADS, HEAD_SIZE), value_lowered.reshape(N_DP, GROUP_LENGTH, KEY_VALUE_HEADS, HEAD_SIZE), segment_index, valid_mask))
    mixed = tokens_f + low_back(matmul(head_outputs.reshape(TOKEN_SLOTS, QUERY_HEADS * HEAD_SIZE), w_out_f))
    ffn_in = lower_precision(rows_normalize(mixed, ffn_gain_f))
    gate = low_back(matmul(ffn_in, w_gate_f))
    up_proj = low_back(matmul(ffn_in, w_up_f))
    hidden = lower_precision(jax.nn.silu(gate) * up_proj)
    return mixed + matmul(hidden, w_down_f)

def reference(tokens, lengths, attn_gain, w_query, key_weight, value_weight, query_gain, key_gain, w_out, ffn_gain, w_gate, w_up, w_down, out_grad):
    segment_index, position, valid_mask = jax.vmap(lambda row_lengths: segments(row_lengths, GROUP_LENGTH))(lengths)
    bound = partial(forward, segment_index=segment_index, position=position, valid_mask=valid_mask)
    result, pullback = jax.vjp(bound, tokens.astype(jnp.float32), attn_gain.astype(jnp.float32), w_query.astype(jnp.float32), key_weight.astype(jnp.float32), value_weight.astype(jnp.float32), query_gain.astype(jnp.float32), key_gain.astype(jnp.float32), w_out.astype(jnp.float32), ffn_gain.astype(jnp.float32), w_gate.astype(jnp.float32), w_up.astype(jnp.float32), w_down.astype(jnp.float32))
    cotangent = jnp.where(valid_mask.reshape(TOKEN_SLOTS)[:, None], out_grad.astype(jnp.float32), jnp.zeros((TOKEN_SLOTS, MODEL_WIDTH), jnp.float32))
    grads = pullback(cotangent)
    return (result.astype(jnp.bfloat16), grads[0], grads[1], grads[2], grads[3], grads[4], grads[5], grads[6], grads[7], grads[8], grads[9], grads[10], grads[11])
```

```python
import jax
import jax.numpy as jnp
from jax import lax
from jax.sharding import PartitionSpec as P

EPSILON = 1e-05
ROPE_BASE = 1000000.0
MASK_FILL = -1e30


def segments(seq_lengths, total_slots):
    ends = jnp.cumsum(seq_lengths)
    starts = ends - seq_lengths
    places = jnp.arange(total_slots, dtype=jnp.int32)
    segment_index = jnp.sum((places[:, None] >= ends[None, :]).astype(jnp.int32), axis=1)
    number = seq_lengths.shape[0]
    chosen = segment_index[:, None] == jnp.arange(number, dtype=jnp.int32)[None, :]
    first_slot = jnp.sum(jnp.where(chosen, starts[None, :], 0), axis=1)
    return (segment_index, places - first_slot, segment_index < number)


def block_mask(segment_index, valid_mask, low_row, high_row, key_count):
    query_places = jnp.arange(low_row, high_row)
    key_places = jnp.arange(key_count)
    causal = key_places[None, :] <= query_places[:, None]
    same = (
        (segment_index[low_row:high_row, None] == segment_index[None, :key_count])
        & valid_mask[low_row:high_row, None]
        & causal
    )
    return same | (key_places[None, :] == query_places[:, None])


def rows_normalize(values, gain_vec):
    inverse = lax.rsqrt(jnp.mean(values * values, axis=-1, keepdims=True) + EPSILON)
    return (values * inverse * gain_vec, inverse)


def norm_back(values, inverse, gain_vec, grad_in):
    scaled = grad_in * gain_vec
    inner_mean = jnp.mean(scaled * values, axis=-1, keepdims=True)
    return (
        inverse * (scaled - values * inverse * inverse * inner_mean),
        grad_in * values * inverse,
    )


def rope_tables(position, width):
    half_width = width // 2
    frequency = ROPE_BASE ** (-(jnp.arange(half_width).astype(jnp.float32) * 2.0 / width))
    angles = position.astype(jnp.float32)[:, None] * frequency[None, :]
    return (jnp.cos(angles)[:, None, :], jnp.sin(angles)[:, None, :])


def apply_rotary(values, cosine_table, sine_table):
    half_width = values.shape[-1] // 2
    first_half = values[..., :half_width]
    second_half = values[..., half_width:]
    return jnp.concatenate(
        [
            first_half * cosine_table - second_half * sine_table,
            second_half * cosine_table + first_half * sine_table,
        ],
        axis=-1,
    )


def unrotate(grad_in, cosine_table, sine_table):
    half_width = grad_in.shape[-1] // 2
    first_half = grad_in[..., :half_width]
    second_half = grad_in[..., half_width:]
    return jnp.concatenate(
        [
            first_half * cosine_table + second_half * sine_table,
            second_half * cosine_table - first_half * sine_table,
        ],
        axis=-1,
    )


def contract_rows(left, right):
    return lax.dot_general(
        left, right, (((0,), (0,)), ((), ())), preferred_element_type=jnp.float32
    )


def contract_cols(left, right):
    return lax.dot_general(
        left, right, (((1,), (1,)), ((), ())), preferred_element_type=jnp.float32
    )


def ring_pos(chip, chips):
    return jnp.where(chip % 2 == 0, chip // 2, chips - 1 - chip // 2)


def ring_chip(pos, chips):
    pos = pos % chips
    return jnp.where(pos < chips // 2, 2 * pos, 2 * (chips - 1 - pos) + 1)


def ring_perms(chips):
    order = list(range(0, chips, 2)) + list(range(1, chips, 2))[::-1]
    right = []
    for place in range(chips):
        for core in range(2):
            right.append((order[place] * 2 + core, order[(place + 1) % chips] * 2 + core))
    return right, [(b, a) for a, b in right], [(i, i ^ 1) for i in range(2 * chips)]


def hops(chips, flip):
    longer = chips // 2
    return (chips - 1 - longer, longer) if flip else (longer, chips - 1 - longer)


def ring_gather(block, flip):
    chips = lax.axis_size("dp") // 2
    right, left, sibling = ring_perms(chips)
    index = lax.axis_index("dp")
    core = index % 2
    place = ring_pos(index // 2, chips)
    count_right, count_left = hops(chips, flip)
    lane = jnp.zeros((chips,) + block.shape, block.dtype)
    lane = lax.dynamic_update_index_in_dim(lane, block, index // 2, 0)
    from_left, from_right = block, block
    for step in range(1, max(count_right, count_left) + 1):
        if step <= count_right:
            from_left = lax.ppermute(from_left, "dp", right)
            lane = lax.dynamic_update_index_in_dim(
                lane, from_left, ring_chip(place - step, chips), 0
            )
        if step <= count_left:
            from_right = lax.ppermute(from_right, "dp", left)
            lane = lax.dynamic_update_index_in_dim(
                lane, from_right, ring_chip(place + step, chips), 0
            )
    other = lax.ppermute(lane, "dp", sibling)
    first = jnp.where(core == 0, lane, other)
    second = jnp.where(core == 0, other, lane)
    return jnp.stack([first, second], axis=1).reshape(2 * chips * block.shape[0], -1)


def ring_scatter(full, flip):
    chips = lax.axis_size("dp") // 2
    right, left, sibling = ring_perms(chips)
    index = lax.axis_index("dp")
    core = index % 2
    place = ring_pos(index // 2, chips)
    count_right, count_left = hops(chips, flip)
    pairs = full.reshape(chips, 2, full.shape[0] // (2 * chips), full.shape[1])
    mine = jnp.where(core == 0, pairs[:, 0], pairs[:, 1])
    theirs = jnp.where(core == 0, pairs[:, 1], pairs[:, 0])
    got = lax.ppermute(theirs, "dp", sibling)

    def chunk(pos):
        chip = ring_chip(pos, chips)
        return lax.dynamic_index_in_dim(mine, chip, 0, keepdims=False).astype(
            jnp.float32
        ) + lax.dynamic_index_in_dim(got, chip, 0, keepdims=False).astype(jnp.float32)

    total = chunk(place)
    for count, perm, sign in ((count_right, right, 1), (count_left, left, -1)):
        received = None
        for step in range(count, 0, -1):
            partial = chunk(place + sign * step)
            if received is not None:
                partial = partial + received.astype(jnp.float32)
            received = lax.ppermute(partial.astype(jnp.bfloat16), "dp", perm)
        if received is not None:
            total = total + received.astype(jnp.float32)
    return total


def shifted(values, shift):
    size = lax.axis_size("tensor")
    return lax.ppermute(values, "tensor", [((i + shift) % size, i) for i in range(size)])


def gather_parts(own):
    return [own] + [shifted(own, k) for k in range(1, lax.axis_size("tensor"))]


def scatter_parts(make_part):
    size = lax.axis_size("tensor")
    arrived = [shifted(make_part(k).astype(jnp.bfloat16), -k) for k in range(1, size)]
    total = make_part(0)
    for part in arrived:
        total = total + part.astype(jnp.float32)
    return total


def to_slots(parts):
    size = len(parts)
    rows = parts[0].shape[0]
    start = ((size - lax.axis_index("tensor")) % size) * rows
    return lax.dynamic_slice_in_dim(jnp.concatenate(parts + parts[:-1], axis=0), start, size * rows, 0)


def part_of(values, k):
    size = lax.axis_size("tensor")
    rows = values.shape[0] // size
    return lax.dynamic_slice_in_dim(
        values, ((lax.axis_index("tensor") + k) % size) * rows, rows, 0
    )


def sum_everywhere(values):
    for name in ("tensor", "dp"):
        size = lax.axis_size(name)
        bit = 1
        while bit < size:
            values = values + lax.ppermute(values, name, [(i, i ^ bit) for i in range(size)])
            bit *= 2
    return values


def per_device(
    tokens,
    lengths,
    attn_gain,
    w_query,
    key_weight,
    value_weight,
    query_gain,
    key_gain,
    w_out,
    ffn_gain,
    w_gate,
    w_up,
    w_down,
    out_grad,
):
    tok_rows = tokens.shape[0]
    group_rows = tok_rows * lax.axis_size("tensor")
    head_dim = query_gain.shape[0]
    kv_heads = key_weight.shape[1] // head_dim
    query_heads = w_query.shape[1] // head_dim
    repeat = query_heads // kv_heads
    blk_rows = min(512, group_rows)
    score_scale = head_dim ** (-0.5)
    segment_index, position, valid_mask = segments(lengths[0], group_rows)
    first_row = lax.axis_index("tensor") * tok_rows
    valid_local = lax.dynamic_slice_in_dim(valid_mask, first_row, tok_rows, 0)
    cosine_table, sine_table = rope_tables(position, head_dim)
    qgain_wide = query_gain.astype(jnp.float32)
    kgain_wide = key_gain.astype(jnp.float32)
    shard_rows = w_query.shape[0]
    qw, kw = w_query.shape[1], key_weight.shape[1]
    token_parts = gather_parts(tokens)
    grad_out = jnp.where(valid_local[:, None], out_grad, jnp.zeros_like(out_grad))
    gain_columns = jnp.concatenate(
        [
            attn_gain[:, None],
            ffn_gain[:, None],
            jnp.zeros((shard_rows, 126), jnp.bfloat16),
        ],
        axis=1,
    )
    attn_pack = ring_gather(
        jnp.concatenate([w_query, key_weight, value_weight, w_out.T, gain_columns], axis=1), False
    )
    wg_all = ring_gather(w_gate, True)
    wu_all = ring_gather(w_up, False)
    wdt_all = ring_gather(w_down.T, True)
    wq_all = attn_pack[:, :qw]
    wk_all = attn_pack[:, qw : qw + kw]
    wv_all = attn_pack[:, qw + kw : qw + 2 * kw]
    wot_all = attn_pack[:, qw + 2 * kw : 2 * qw + 2 * kw]
    attn_gain_all = attn_pack[:, 2 * qw + 2 * kw]
    ffn_gain_all = attn_pack[:, 2 * qw + 2 * kw + 1]
    grad_parts = gather_parts(grad_out)
    tokens_wide = tokens.astype(jnp.float32)
    attn_inv = lax.rsqrt(jnp.mean(tokens_wide * tokens_wide, axis=-1, keepdims=True) + EPSILON)
    attn_rows = rows_normalize(
        to_slots(token_parts).astype(jnp.float32), attn_gain_all.astype(jnp.float32)
    )[0].astype(jnp.bfloat16)
    query_raw = jnp.dot(attn_rows, wq_all, preferred_element_type=jnp.float32).reshape(
        group_rows, query_heads, head_dim
    )
    key_unrotated = jnp.dot(attn_rows, wk_all, preferred_element_type=jnp.float32).reshape(
        group_rows, kv_heads, head_dim
    )
    value_lowered = (
        jnp.dot(attn_rows, wv_all, preferred_element_type=jnp.float32)
        .astype(jnp.bfloat16)
        .reshape(group_rows, kv_heads, head_dim)
    )
    query_normed, query_inv = rows_normalize(query_raw, qgain_wide)
    key_normed, key_inv = rows_normalize(key_unrotated, kgain_wide)
    query_low = apply_rotary(query_normed, cosine_table, sine_table).astype(jnp.bfloat16)
    key_low = apply_rotary(key_normed, cosine_table, sine_table).astype(jnp.bfloat16)
    query_grouped = query_low.reshape(group_rows, kv_heads, repeat, head_dim)
    outputs = []
    kept_stats = []
    for number in range(group_rows // blk_rows):
        low_row = number * blk_rows
        high_row = low_row + blk_rows
        allowed = block_mask(segment_index, valid_mask, low_row, high_row, high_row)
        scores = (
            jnp.einsum(
                "qgrd,kgd->grqk",
                query_grouped[low_row:high_row],
                key_low[:high_row],
                preferred_element_type=jnp.float32,
            )
            * score_scale
        )
        scores = jnp.where(allowed[None, None], scores, MASK_FILL)
        row_peak = jnp.max(scores, axis=-1, keepdims=True)
        exp_terms = jnp.exp(scores - row_peak)
        row_total = jnp.sum(exp_terms, axis=-1, keepdims=True)
        probs_low = (exp_terms / row_total).astype(jnp.bfloat16)
        outputs.append(
            jnp.einsum(
                "grqk,kgd->qgrd",
                probs_low,
                value_lowered[:high_row],
                preferred_element_type=jnp.float32,
            )
        )
        kept_stats.append((row_peak, row_total))
    heads_low = (
        jnp.concatenate(outputs, axis=0)
        .reshape(group_rows, query_heads * head_dim)
        .astype(jnp.bfloat16)
    )
    mixed = tokens_wide + scatter_parts(lambda k: contract_cols(part_of(heads_low, k), wot_all))
    ffn_in, ffn_inv = rows_normalize(mixed, ffn_gain_all.astype(jnp.float32))
    ffn_parts = gather_parts(ffn_in.astype(jnp.bfloat16))
    gates, ups, hiddens, grad_gates, grad_ups = [], [], [], [], []
    for ffn_rows, grad_rows in zip(ffn_parts, grad_parts):
        gate = jnp.dot(ffn_rows, wg_all, preferred_element_type=jnp.float32)
        up_proj = jnp.dot(ffn_rows, wu_all, preferred_element_type=jnp.float32)
        grad_hidden = jnp.dot(grad_rows, wdt_all, preferred_element_type=jnp.float32)
        sigmoid_gate = jax.nn.sigmoid(gate)
        hiddens.append((gate * sigmoid_gate * up_proj).astype(jnp.bfloat16))
        grad_ups.append((grad_hidden * gate * sigmoid_gate).astype(jnp.bfloat16))
        grad_gates.append(
            (
                grad_hidden * up_proj * sigmoid_gate * (1.0 + gate * (1.0 - sigmoid_gate))
            ).astype(jnp.bfloat16)
        )
    grad_ffn_in = scatter_parts(
        lambda k: contract_cols(grad_gates[k], wg_all) + contract_cols(grad_ups[k], wu_all)
    )
    back_mixed, ffn_gain_part = norm_back(
        mixed, ffn_inv, ffn_gain_all.astype(jnp.float32), grad_ffn_in
    )
    grad_mixed = grad_out.astype(jnp.float32) + back_mixed
    mixed_parts = gather_parts(grad_mixed.astype(jnp.bfloat16))
    result = mixed + scatter_parts(lambda k: contract_cols(hiddens[k], wdt_all))
    output = result.astype(jnp.bfloat16)
    ffn_cat = jnp.concatenate(ffn_parts, axis=0)
    grad_cat = jnp.concatenate(grad_parts, axis=0)
    ffn_sums = (
        ring_scatter(
            contract_rows(ffn_cat, jnp.concatenate(grad_gates, axis=0)).astype(jnp.bfloat16), False
        ),
        ring_scatter(
            contract_rows(ffn_cat, jnp.concatenate(grad_ups, axis=0)).astype(jnp.bfloat16), True
        ),
        ring_scatter(
            contract_rows(grad_cat, jnp.concatenate(hiddens, axis=0)).astype(jnp.bfloat16), False
        ).T,
    )
    grad_heads = to_slots(
        [
            jnp.dot(rows, wot_all, preferred_element_type=jnp.float32).astype(jnp.bfloat16)
            for rows in mixed_parts
        ]
    ).reshape(group_rows, kv_heads, repeat, head_dim)
    grad_wot = contract_rows(to_slots(mixed_parts), heads_low)
    grad_query_parts = []
    grad_key = jnp.zeros((group_rows, kv_heads, head_dim), jnp.float32)
    grad_value = jnp.zeros((group_rows, kv_heads, head_dim), jnp.float32)
    for number in range(group_rows // blk_rows):
        low_row = number * blk_rows
        high_row = low_row + blk_rows
        row_peak, row_total = kept_stats[number]
        allowed = block_mask(segment_index, valid_mask, low_row, high_row, high_row)
        scores = (
            jnp.einsum(
                "qgrd,kgd->grqk",
                query_grouped[low_row:high_row],
                key_low[:high_row],
                preferred_element_type=jnp.float32,
            )
            * score_scale
        )
        scores = jnp.where(allowed[None, None], scores, MASK_FILL)
        probs_wide = jnp.exp(scores - row_peak) / row_total
        probs_low = probs_wide.astype(jnp.bfloat16)
        grad_probs = jnp.einsum(
            "qgrd,kgd->grqk",
            grad_heads[low_row:high_row],
            value_lowered[:high_row],
            preferred_element_type=jnp.float32,
        )
        inner_sum = jnp.sum(probs_wide * grad_probs, axis=-1, keepdims=True)
        grad_scores = (probs_wide * (grad_probs - inner_sum)).astype(jnp.bfloat16)
        grad_query_parts.append(
            jnp.einsum(
                "grqk,kgd->qgrd",
                grad_scores,
                key_low[:high_row],
                preferred_element_type=jnp.float32,
            )
            * score_scale
        )
        grad_key = grad_key.at[:high_row].add(
            jnp.einsum(
                "grqk,qgrd->kgd",
                grad_scores,
                query_grouped[low_row:high_row],
                preferred_element_type=jnp.float32,
            )
            * score_scale
        )
        grad_value = grad_value.at[:high_row].add(
            jnp.einsum(
                "grqk,qgrd->kgd",
                probs_low,
                grad_heads[low_row:high_row],
                preferred_element_type=jnp.float32,
            )
        )
    grad_query_all = jnp.concatenate(grad_query_parts, axis=0).reshape(
        group_rows, query_heads, head_dim
    )
    grad_query_raw, qgain_terms = norm_back(
        query_raw, query_inv, qgain_wide, unrotate(grad_query_all, cosine_table, sine_table)
    )
    grad_key_raw, kgain_terms = norm_back(
        key_unrotated, key_inv, kgain_wide, unrotate(grad_key, cosine_table, sine_table)
    )
    grad_query_low = grad_query_raw.reshape(group_rows, query_heads * head_dim).astype(jnp.bfloat16)
    grad_key_low = grad_key_raw.reshape(group_rows, kv_heads * head_dim).astype(jnp.bfloat16)
    grad_value_low = grad_value.reshape(group_rows, kv_heads * head_dim).astype(jnp.bfloat16)
    grad_wq = contract_rows(attn_rows, grad_query_low)
    grad_wk = contract_rows(attn_rows, grad_key_low)
    grad_wv = contract_rows(attn_rows, grad_value_low)
    grad_attn_in = scatter_parts(
        lambda k: contract_cols(part_of(grad_query_low, k), wq_all)
        + contract_cols(part_of(grad_key_low, k), wk_all)
        + contract_cols(part_of(grad_value_low, k), wv_all)
    )
    back_tokens, attn_gain_part = norm_back(
        tokens_wide, attn_inv, attn_gain_all.astype(jnp.float32), grad_attn_in
    )
    input_grad = grad_mixed + back_tokens
    attn_pack_sum = ring_scatter(
        jnp.concatenate([grad_wq, grad_wk, grad_wv, grad_wot], axis=1).astype(jnp.bfloat16), True
    )
    attn_sums = (
        attn_pack_sum[:, :qw],
        attn_pack_sum[:, qw : qw + kw],
        attn_pack_sum[:, qw + kw : qw + 2 * kw],
        attn_pack_sum[:, qw + 2 * kw :].T,
    )
    width = tokens.shape[1]
    early = sum_everywhere(
        jnp.concatenate(
            [
                jnp.sum(ffn_gain_part, axis=0),
                jnp.sum(qgain_terms, axis=(0, 1)),
                jnp.sum(kgain_terms, axis=(0, 1)),
            ]
        )
    )
    gain_sums = (
        sum_everywhere(jnp.sum(attn_gain_part, axis=0)),
        early[:width],
        early[width : width + head_dim],
        early[width + head_dim :],
    )
    gain_shard = attn_gain.shape[0]
    gain_start = lax.axis_index("dp") * gain_shard
    attn_gain_grad = lax.dynamic_slice_in_dim(gain_sums[0], gain_start, gain_shard, 0)
    ffn_gain_grad = lax.dynamic_slice_in_dim(gain_sums[1], gain_start, gain_shard, 0)
    return (
        output,
        input_grad,
        attn_gain_grad,
        attn_sums[0],
        attn_sums[1],
        attn_sums[2],
        gain_sums[2],
        gain_sums[3],
        attn_sums[3],
        ffn_gain_grad,
        ffn_sums[0],
        ffn_sums[1],
        ffn_sums[2],
    )


def solution(mesh):
    in_specs = (
        P(("dp", "tensor"), None),
        P("dp", None),
        P("dp"),
        P("dp", "tensor"),
        P("dp", "tensor"),
        P("dp", "tensor"),
        P(),
        P(),
        P("tensor", "dp"),
        P("dp"),
        P("dp", "tensor"),
        P("dp", "tensor"),
        P("tensor", "dp"),
        P(("dp", "tensor"), None),
    )
    out_specs = (
        P(("dp", "tensor"), None),
        P(("dp", "tensor"), None),
        P("dp"),
        P("dp", "tensor"),
        P("dp", "tensor"),
        P("dp", "tensor"),
        P(),
        P(),
        P("tensor", "dp"),
        P("dp"),
        P("dp", "tensor"),
        P("dp", "tensor"),
        P("tensor", "dp"),
    )
    return jax.shard_map(
        per_device, mesh=mesh, in_specs=in_specs, out_specs=out_specs, check_vma=False
    )
```

```python
import jax
import jax.numpy as jnp
from jax import lax
from jax.sharding import PartitionSpec as P

EPSILON = 1e-05
ROPE_BASE = 1000000.0
MASK_FILL = -1e30


def segments(seq_lengths, total_slots):
    ends = jnp.cumsum(seq_lengths)
    starts = ends - seq_lengths
    places = jnp.arange(total_slots, dtype=jnp.int32)
    segment_index = jnp.sum((places[:, None] >= ends[None, :]).astype(jnp.int32), axis=1)
    number = seq_lengths.shape[0]
    chosen = segment_index[:, None] == jnp.arange(number, dtype=jnp.int32)[None, :]
    first_slot = jnp.sum(jnp.where(chosen, starts[None, :], 0), axis=1)
    return (segment_index, places - first_slot, segment_index < number)


def block_mask(segment_index, valid_mask, low_row, high_row, key_count):
    query_places = jnp.arange(low_row, high_row)
    key_places = jnp.arange(key_count)
    causal = key_places[None, :] <= query_places[:, None]
    same = (
        (segment_index[low_row:high_row, None] == segment_index[None, :key_count])
        & valid_mask[low_row:high_row, None]
        & causal
    )
    return same | (key_places[None, :] == query_places[:, None])


def rows_normalize(values, gain_vec):
    inverse = lax.rsqrt(jnp.mean(values * values, axis=-1, keepdims=True) + EPSILON)
    return (values * inverse * gain_vec, inverse)


def norm_back(values, inverse, gain_vec, grad_in):
    scaled = grad_in * gain_vec
    inner_mean = jnp.mean(scaled * values, axis=-1, keepdims=True)
    return (
        inverse * (scaled - values * inverse * inverse * inner_mean),
        grad_in * values * inverse,
    )


def rope_tables(position, width):
    half_width = width // 2
    frequency = ROPE_BASE ** (-(jnp.arange(half_width).astype(jnp.float32) * 2.0 / width))
    angles = position.astype(jnp.float32)[:, None] * frequency[None, :]
    return (jnp.cos(angles)[:, None, :], jnp.sin(angles)[:, None, :])


def apply_rotary(values, cosine_table, sine_table):
    half_width = values.shape[-1] // 2
    first_half = values[..., :half_width]
    second_half = values[..., half_width:]
    return jnp.concatenate(
        [
            first_half * cosine_table - second_half * sine_table,
            second_half * cosine_table + first_half * sine_table,
        ],
        axis=-1,
    )


def unrotate(grad_in, cosine_table, sine_table):
    half_width = grad_in.shape[-1] // 2
    first_half = grad_in[..., :half_width]
    second_half = grad_in[..., half_width:]
    return jnp.concatenate(
        [
            first_half * cosine_table + second_half * sine_table,
            second_half * cosine_table - first_half * sine_table,
        ],
        axis=-1,
    )


def contract_rows(left, right):
    return lax.dot_general(
        left, right, (((0,), (0,)), ((), ())), preferred_element_type=jnp.float32
    )


def contract_cols(left, right):
    return lax.dot_general(
        left, right, (((1,), (1,)), ((), ())), preferred_element_type=jnp.float32
    )


def ring_pos(chip, chips):
    return jnp.where(chip % 2 == 0, chip // 2, chips - 1 - chip // 2)


def ring_chip(pos, chips):
    pos = pos % chips
    return jnp.where(pos < chips // 2, 2 * pos, 2 * (chips - 1 - pos) + 1)


def ring_perms(chips):
    order = list(range(0, chips, 2)) + list(range(1, chips, 2))[::-1]
    right = []
    for place in range(chips):
        for core in range(2):
            right.append((order[place] * 2 + core, order[(place + 1) % chips] * 2 + core))
    return right, [(b, a) for a, b in right], [(i, i ^ 1) for i in range(2 * chips)]


def hops(chips, flip):
    longer = chips // 2
    return (chips - 1 - longer, longer) if flip else (longer, chips - 1 - longer)


def tie(*values):
    return lax.optimization_barrier(values)


def ring_gather(block, flip):
    chips = lax.axis_size("dp") // 2
    right, left, sibling = ring_perms(chips)
    index = lax.axis_index("dp")
    core = index % 2
    place = ring_pos(index // 2, chips)
    count_right, count_left = hops(chips, flip)
    steps = max(count_right, count_left)
    whole = jnp.zeros((chips, 2) + block.shape, block.dtype)

    def put(whole, value, pos, side):
        return lax.dynamic_update_slice(
            whole, value[None, None], (ring_chip(pos, chips), side, 0, 0)
        )

    whole = put(whole, block, place, core)
    held, places = [block], [place]
    from_left, from_right = block, block
    for step in range(1, steps + 1):
        arrived = []
        if step <= count_right:
            from_left = lax.ppermute(from_left, "dp", right)
            arrived.append((from_left, place - step))
        if step <= count_left:
            from_right = lax.ppermute(from_right, "dp", left)
            arrived.append((from_right, place + step))
        proceed = yield [value for value, _ in arrived]
        if proceed is not None:
            arrived = [(value, pos) for value, (_, pos) in zip(proceed, arrived)]
            if step <= count_right:
                from_left = proceed[0]
            if step <= count_left:
                from_right = proceed[-1]
        for value, pos in arrived:
            whole = put(whole, value, pos, core)
            held.append(value)
            places.append(pos)
        if step == (steps + 1) // 2 or step == steps:
            other = lax.ppermute(jnp.stack(held), "dp", sibling)
            for number, pos in enumerate(places):
                whole = put(whole, other[number], pos, 1 - core)
            held, places = [], []
    return whole.reshape(2 * chips * block.shape[0], block.shape[1])


def ring_scatter(arrays, flip):
    chips = lax.axis_size("dp") // 2
    right, left, sibling = ring_perms(chips)
    index = lax.axis_index("dp")
    core = index % 2
    place = ring_pos(index // 2, chips)
    count_right, count_left = hops(chips, flip)
    pairs = [v.reshape(chips, 2, v.shape[0] // (2 * chips), v.shape[1]) for v in arrays]
    theirs = jnp.concatenate(
        [lax.dynamic_index_in_dim(v, 1 - core, 1, keepdims=False) for v in pairs], axis=2
    )
    got = lax.ppermute(theirs, "dp", sibling)

    def chunk(pos):
        chip = ring_chip(pos, chips)
        own = jnp.concatenate(
            [
                lax.dynamic_slice(v, (chip, core, 0, 0), (1, 1) + v.shape[2:])[0, 0]
                for v in pairs
            ],
            axis=1,
        )
        return own.astype(jnp.float32) + lax.dynamic_index_in_dim(
            got, chip, 0, keepdims=False
        ).astype(jnp.float32)

    from_left, from_right = None, None
    for step in range(max(count_right, count_left), 0, -1):
        sends = []
        if step <= count_right:
            part = chunk(place + step)
            if from_left is not None:
                part = part + from_left.astype(jnp.float32)
            sends.append(part.astype(jnp.bfloat16))
        if step <= count_left:
            part = chunk(place - step)
            if from_right is not None:
                part = part + from_right.astype(jnp.float32)
            sends.append(part.astype(jnp.bfloat16))
        proceed = yield sends
        if proceed is not None:
            sends = proceed
        if step <= count_right:
            from_left = lax.ppermute(sends[0], "dp", right)
        if step <= count_left:
            from_right = lax.ppermute(sends[-1], "dp", left)
    total = chunk(place)
    for part in (from_left, from_right):
        if part is not None:
            total = total + part.astype(jnp.float32)
    return total


class Steps:
    def __init__(self, ring):
        self.ring = ring
        self.waiting = next(ring)
        self.result = None

    def advance(self, value):
        if self.waiting is None:
            return value
        value, *values = tie(value, *self.waiting)
        try:
            self.waiting = self.ring.send(values)
        except StopIteration as end:
            self.waiting, self.result = None, end.value
        return value

    def finish(self):
        while self.waiting is not None:
            try:
                self.waiting = self.ring.send(None)
            except StopIteration as end:
                self.waiting, self.result = None, end.value
        return self.result


def shifted(values, shift):
    size = lax.axis_size("tensor")
    return lax.ppermute(values, "tensor", [((i + shift) % size, i) for i in range(size)])


def gather_parts(own):
    return [own] + [shifted(own, k) for k in range(1, lax.axis_size("tensor"))]


def scatter_parts(make_part):
    size = lax.axis_size("tensor")
    arrived = [shifted(make_part(k).astype(jnp.bfloat16), -k) for k in range(1, size)]
    total = make_part(0)
    for part in arrived:
        total = total + part.astype(jnp.float32)
    return total


def to_slots(parts):
    size = len(parts)
    rows = parts[0].shape[0]
    start = ((size - lax.axis_index("tensor")) % size) * rows
    return lax.dynamic_slice_in_dim(jnp.concatenate(parts + parts[:-1], axis=0), start, size * rows, 0)


def part_of(values, k):
    size = lax.axis_size("tensor")
    rows = values.shape[0] // size
    return lax.dynamic_slice_in_dim(
        values, ((lax.axis_index("tensor") + k) % size) * rows, rows, 0
    )


def sum_everywhere(values):
    for name in ("tensor", "dp"):
        size = lax.axis_size(name)
        bit = 1
        while bit < size:
            values = values + lax.ppermute(values, name, [(i, i ^ bit) for i in range(size)])
            bit *= 2
    return values


def per_device(
    tokens,
    lengths,
    attn_gain,
    w_query,
    key_weight,
    value_weight,
    query_gain,
    key_gain,
    w_out,
    ffn_gain,
    w_gate,
    w_up,
    w_down,
    out_grad,
):
    tok_rows = tokens.shape[0]
    group_rows = tok_rows * lax.axis_size("tensor")
    head_dim = query_gain.shape[0]
    kv_heads = key_weight.shape[1] // head_dim
    query_heads = w_query.shape[1] // head_dim
    repeat = query_heads // kv_heads
    blk_rows = min(512, group_rows)
    score_scale = head_dim ** (-0.5)
    segment_index, position, valid_mask = segments(lengths[0], group_rows)
    first_row = lax.axis_index("tensor") * tok_rows
    valid_local = lax.dynamic_slice_in_dim(valid_mask, first_row, tok_rows, 0)
    cosine_table, sine_table = rope_tables(position, head_dim)
    qgain_wide = query_gain.astype(jnp.float32)
    kgain_wide = key_gain.astype(jnp.float32)
    shard_rows = w_query.shape[0]
    qw, kw = w_query.shape[1], key_weight.shape[1]
    token_parts = gather_parts(tokens)
    grad_out = jnp.where(valid_local[:, None], out_grad, jnp.zeros_like(out_grad))
    gain_columns = jnp.concatenate(
        [
            attn_gain[:, None],
            ffn_gain[:, None],
            jnp.zeros((shard_rows, 126), jnp.bfloat16),
        ],
        axis=1,
    )
    attn_pack = Steps(
        ring_gather(
            jnp.concatenate([w_query, key_weight, value_weight, w_out.T, gain_columns], axis=1),
            False,
        )
    ).finish()
    ffn_block = jnp.concatenate([w_gate, w_up, w_down.T], axis=1)
    attn_pack, ffn_block = tie(attn_pack, ffn_block)
    ffn_ring = Steps(ring_gather(ffn_block, True))
    fw = w_gate.shape[1]
    wq_all = attn_pack[:, :qw]
    wk_all = attn_pack[:, qw : qw + kw]
    wv_all = attn_pack[:, qw + kw : qw + 2 * kw]
    wot_all = attn_pack[:, qw + 2 * kw : 2 * qw + 2 * kw]
    attn_gain_all = attn_pack[:, 2 * qw + 2 * kw]
    ffn_gain_all = attn_pack[:, 2 * qw + 2 * kw + 1]
    grad_parts = gather_parts(grad_out)
    tokens_wide = tokens.astype(jnp.float32)
    attn_inv = lax.rsqrt(jnp.mean(tokens_wide * tokens_wide, axis=-1, keepdims=True) + EPSILON)
    attn_rows = rows_normalize(
        to_slots(token_parts).astype(jnp.float32), attn_gain_all.astype(jnp.float32)
    )[0].astype(jnp.bfloat16)
    query_raw = jnp.dot(attn_rows, wq_all, preferred_element_type=jnp.float32).reshape(
        group_rows, query_heads, head_dim
    )
    key_unrotated = jnp.dot(attn_rows, wk_all, preferred_element_type=jnp.float32).reshape(
        group_rows, kv_heads, head_dim
    )
    value_lowered = (
        jnp.dot(attn_rows, wv_all, preferred_element_type=jnp.float32)
        .astype(jnp.bfloat16)
        .reshape(group_rows, kv_heads, head_dim)
    )
    query_normed, query_inv = rows_normalize(query_raw, qgain_wide)
    key_normed, key_inv = rows_normalize(key_unrotated, kgain_wide)
    query_low = apply_rotary(query_normed, cosine_table, sine_table).astype(jnp.bfloat16)
    key_low = apply_rotary(key_normed, cosine_table, sine_table).astype(jnp.bfloat16)
    query_low = ffn_ring.advance(query_low)
    query_grouped = query_low.reshape(group_rows, kv_heads, repeat, head_dim)
    outputs = []
    kept_stats = []
    for number in range(group_rows // blk_rows):
        low_row = number * blk_rows
        high_row = low_row + blk_rows
        allowed = block_mask(segment_index, valid_mask, low_row, high_row, high_row)
        scores = (
            jnp.einsum(
                "qgrd,kgd->grqk",
                query_grouped[low_row:high_row],
                key_low[:high_row],
                preferred_element_type=jnp.float32,
            )
            * score_scale
        )
        scores = jnp.where(allowed[None, None], scores, MASK_FILL)
        row_peak = jnp.max(scores, axis=-1, keepdims=True)
        exp_terms = jnp.exp(scores - row_peak)
        row_total = jnp.sum(exp_terms, axis=-1, keepdims=True)
        probs_low = (exp_terms / row_total).astype(jnp.bfloat16)
        outputs.append(
            jnp.einsum(
                "grqk,kgd->qgrd",
                probs_low,
                value_lowered[:high_row],
                preferred_element_type=jnp.float32,
            )
        )
        kept_stats.append((row_peak, row_total))
        outputs[-1] = ffn_ring.advance(outputs[-1])
    heads_low = (
        jnp.concatenate(outputs, axis=0)
        .reshape(group_rows, query_heads * head_dim)
        .astype(jnp.bfloat16)
    )
    mixed = tokens_wide + scatter_parts(lambda k: contract_cols(part_of(heads_low, k), wot_all))
    ffn_in, ffn_inv = rows_normalize(mixed, ffn_gain_all.astype(jnp.float32))
    ffn_pack = ffn_ring.finish()
    wg_all, wu_all, wdt_all = ffn_pack[:, :fw], ffn_pack[:, fw : 2 * fw], ffn_pack[:, 2 * fw :]
    ffn_parts = gather_parts(ffn_in.astype(jnp.bfloat16))
    gates, ups, hiddens, grad_gates, grad_ups = [], [], [], [], []
    for ffn_rows, grad_rows in zip(ffn_parts, grad_parts):
        gate = jnp.dot(ffn_rows, wg_all, preferred_element_type=jnp.float32)
        up_proj = jnp.dot(ffn_rows, wu_all, preferred_element_type=jnp.float32)
        grad_hidden = jnp.dot(grad_rows, wdt_all, preferred_element_type=jnp.float32)
        sigmoid_gate = jax.nn.sigmoid(gate)
        hiddens.append((gate * sigmoid_gate * up_proj).astype(jnp.bfloat16))
        grad_ups.append((grad_hidden * gate * sigmoid_gate).astype(jnp.bfloat16))
        grad_gates.append(
            (
                grad_hidden * up_proj * sigmoid_gate * (1.0 + gate * (1.0 - sigmoid_gate))
            ).astype(jnp.bfloat16)
        )
    grad_ffn_in = scatter_parts(
        lambda k: contract_cols(grad_gates[k], wg_all) + contract_cols(grad_ups[k], wu_all)
    )
    back_mixed, ffn_gain_part = norm_back(
        mixed, ffn_inv, ffn_gain_all.astype(jnp.float32), grad_ffn_in
    )
    grad_mixed = grad_out.astype(jnp.float32) + back_mixed
    mixed_parts = gather_parts(grad_mixed.astype(jnp.bfloat16))
    result = mixed + scatter_parts(lambda k: contract_cols(hiddens[k], wdt_all))
    output = result.astype(jnp.bfloat16)
    ffn_cat = jnp.concatenate(ffn_parts, axis=0)
    grad_cat = jnp.concatenate(grad_parts, axis=0)
    ffn_sum_ring = Steps(
        ring_scatter(
            [
                contract_rows(ffn_cat, jnp.concatenate(grad_gates, axis=0)).astype(jnp.bfloat16),
                contract_rows(ffn_cat, jnp.concatenate(grad_ups, axis=0)).astype(jnp.bfloat16),
                contract_rows(grad_cat, jnp.concatenate(hiddens, axis=0)).astype(jnp.bfloat16),
            ],
            False,
        )
    )
    grad_heads = to_slots(
        [
            jnp.dot(rows, wot_all, preferred_element_type=jnp.float32).astype(jnp.bfloat16)
            for rows in mixed_parts
        ]
    ).reshape(group_rows, kv_heads, repeat, head_dim)
    grad_wot = contract_rows(to_slots(mixed_parts), heads_low)
    grad_query_parts = []
    grad_key = jnp.zeros((group_rows, kv_heads, head_dim), jnp.float32)
    grad_value = jnp.zeros((group_rows, kv_heads, head_dim), jnp.float32)
    for number in range(group_rows // blk_rows):
        low_row = number * blk_rows
        high_row = low_row + blk_rows
        row_peak, row_total = kept_stats[number]
        row_peak = ffn_sum_ring.advance(row_peak)
        allowed = block_mask(segment_index, valid_mask, low_row, high_row, high_row)
        scores = (
            jnp.einsum(
                "qgrd,kgd->grqk",
                query_grouped[low_row:high_row],
                key_low[:high_row],
                preferred_element_type=jnp.float32,
            )
            * score_scale
        )
        scores = jnp.where(allowed[None, None], scores, MASK_FILL)
        probs_wide = jnp.exp(scores - row_peak) / row_total
        probs_low = probs_wide.astype(jnp.bfloat16)
        grad_probs = jnp.einsum(
            "qgrd,kgd->grqk",
            grad_heads[low_row:high_row],
            value_lowered[:high_row],
            preferred_element_type=jnp.float32,
        )
        inner_sum = jnp.sum(probs_wide * grad_probs, axis=-1, keepdims=True)
        grad_scores = (probs_wide * (grad_probs - inner_sum)).astype(jnp.bfloat16)
        grad_scores = ffn_sum_ring.advance(grad_scores)
        grad_query_parts.append(
            jnp.einsum(
                "grqk,kgd->qgrd",
                grad_scores,
                key_low[:high_row],
                preferred_element_type=jnp.float32,
            )
            * score_scale
        )
        grad_key = grad_key.at[:high_row].add(
            jnp.einsum(
                "grqk,qgrd->kgd",
                grad_scores,
                query_grouped[low_row:high_row],
                preferred_element_type=jnp.float32,
            )
            * score_scale
        )
        grad_value = grad_value.at[:high_row].add(
            jnp.einsum(
                "grqk,qgrd->kgd",
                probs_low,
                grad_heads[low_row:high_row],
                preferred_element_type=jnp.float32,
            )
        )
    grad_query_all = jnp.concatenate(grad_query_parts, axis=0).reshape(
        group_rows, query_heads, head_dim
    )
    grad_query_raw, qgain_terms = norm_back(
        query_raw, query_inv, qgain_wide, unrotate(grad_query_all, cosine_table, sine_table)
    )
    grad_key_raw, kgain_terms = norm_back(
        key_unrotated, key_inv, kgain_wide, unrotate(grad_key, cosine_table, sine_table)
    )
    grad_query_low = grad_query_raw.reshape(group_rows, query_heads * head_dim).astype(jnp.bfloat16)
    grad_key_low = grad_key_raw.reshape(group_rows, kv_heads * head_dim).astype(jnp.bfloat16)
    grad_value_low = grad_value.reshape(group_rows, kv_heads * head_dim).astype(jnp.bfloat16)
    grad_wq = contract_rows(attn_rows, grad_query_low)
    grad_wk = contract_rows(attn_rows, grad_key_low)
    grad_wv = contract_rows(attn_rows, grad_value_low)
    grad_attn_in = scatter_parts(
        lambda k: contract_cols(part_of(grad_query_low, k), wq_all)
        + contract_cols(part_of(grad_key_low, k), wk_all)
        + contract_cols(part_of(grad_value_low, k), wv_all)
    )
    back_tokens, attn_gain_part = norm_back(
        tokens_wide, attn_inv, attn_gain_all.astype(jnp.float32), grad_attn_in
    )
    input_grad = grad_mixed + back_tokens
    ffn_sum = ffn_sum_ring.finish()
    ffn_sums = (ffn_sum[:, :fw], ffn_sum[:, fw : 2 * fw], ffn_sum[:, 2 * fw :].T)
    attn_pack_sum = Steps(
        ring_scatter(
            [v.astype(jnp.bfloat16) for v in (grad_wq, grad_wk, grad_wv, grad_wot)], True
        )
    ).finish()
    attn_sums = (
        attn_pack_sum[:, :qw],
        attn_pack_sum[:, qw : qw + kw],
        attn_pack_sum[:, qw + kw : qw + 2 * kw],
        attn_pack_sum[:, qw + 2 * kw :].T,
    )
    width = tokens.shape[1]
    early = sum_everywhere(
        jnp.concatenate(
            [
                jnp.sum(ffn_gain_part, axis=0),
                jnp.sum(qgain_terms, axis=(0, 1)),
                jnp.sum(kgain_terms, axis=(0, 1)),
            ]
        )
    )
    gain_sums = (
        sum_everywhere(jnp.sum(attn_gain_part, axis=0)),
        early[:width],
        early[width : width + head_dim],
        early[width + head_dim :],
    )
    gain_shard = attn_gain.shape[0]
    gain_start = lax.axis_index("dp") * gain_shard
    attn_gain_grad = lax.dynamic_slice_in_dim(gain_sums[0], gain_start, gain_shard, 0)
    ffn_gain_grad = lax.dynamic_slice_in_dim(gain_sums[1], gain_start, gain_shard, 0)
    return (
        output,
        input_grad,
        attn_gain_grad,
        attn_sums[0],
        attn_sums[1],
        attn_sums[2],
        gain_sums[2],
        gain_sums[3],
        attn_sums[3],
        ffn_gain_grad,
        ffn_sums[0],
        ffn_sums[1],
        ffn_sums[2],
    )


def solution(mesh):
    in_specs = (
        P(("dp", "tensor"), None),
        P("dp", None),
        P("dp"),
        P("dp", "tensor"),
        P("dp", "tensor"),
        P("dp", "tensor"),
        P(),
        P(),
        P("tensor", "dp"),
        P("dp"),
        P("dp", "tensor"),
        P("dp", "tensor"),
        P("tensor", "dp"),
        P(("dp", "tensor"), None),
    )
    out_specs = (
        P(("dp", "tensor"), None),
        P(("dp", "tensor"), None),
        P("dp"),
        P("dp", "tensor"),
        P("dp", "tensor"),
        P("dp", "tensor"),
        P(),
        P(),
        P("tensor", "dp"),
        P("dp"),
        P("dp", "tensor"),
        P("dp", "tensor"),
        P("tensor", "dp"),
    )
    return jax.shard_map(
        per_device, mesh=mesh, in_specs=in_specs, out_specs=out_specs, check_vma=False
    )
```

```python
import jax
import jax.numpy as jnp
from jax import lax
from jax.sharding import PartitionSpec as P

EPSILON = 1e-05
ROPE_BASE = 1000000.0
MASK_FILL = -1e30


def segments(seq_lengths, total_slots):
    ends = jnp.cumsum(seq_lengths)
    starts = ends - seq_lengths
    places = jnp.arange(total_slots, dtype=jnp.int32)
    segment_index = jnp.sum((places[:, None] >= ends[None, :]).astype(jnp.int32), axis=1)
    number = seq_lengths.shape[0]
    chosen = segment_index[:, None] == jnp.arange(number, dtype=jnp.int32)[None, :]
    first_slot = jnp.sum(jnp.where(chosen, starts[None, :], 0), axis=1)
    return (segment_index, places - first_slot, segment_index < number)


def block_mask(segment_index, valid_mask, low_row, high_row, key_count):
    query_places = jnp.arange(low_row, high_row)
    key_places = jnp.arange(key_count)
    causal = key_places[None, :] <= query_places[:, None]
    same = (
        (segment_index[low_row:high_row, None] == segment_index[None, :key_count])
        & valid_mask[low_row:high_row, None]
        & causal
    )
    return same | (key_places[None, :] == query_places[:, None])


def rows_normalize(values, gain_vec):
    inverse = lax.rsqrt(jnp.mean(values * values, axis=-1, keepdims=True) + EPSILON)
    return (values * inverse * gain_vec, inverse)


def norm_back(values, inverse, gain_vec, grad_in):
    scaled = grad_in * gain_vec
    inner_mean = jnp.mean(scaled * values, axis=-1, keepdims=True)
    return (
        inverse * (scaled - values * inverse * inverse * inner_mean),
        grad_in * values * inverse,
    )


def rope_tables(position, width):
    half_width = width // 2
    frequency = ROPE_BASE ** (-(jnp.arange(half_width).astype(jnp.float32) * 2.0 / width))
    angles = position.astype(jnp.float32)[:, None] * frequency[None, :]
    return (jnp.cos(angles)[:, None, :], jnp.sin(angles)[:, None, :])


def apply_rotary(values, cosine_table, sine_table):
    half_width = values.shape[-1] // 2
    first_half = values[..., :half_width]
    second_half = values[..., half_width:]
    return jnp.concatenate(
        [
            first_half * cosine_table - second_half * sine_table,
            second_half * cosine_table + first_half * sine_table,
        ],
        axis=-1,
    )


def unrotate(grad_in, cosine_table, sine_table):
    half_width = grad_in.shape[-1] // 2
    first_half = grad_in[..., :half_width]
    second_half = grad_in[..., half_width:]
    return jnp.concatenate(
        [
            first_half * cosine_table + second_half * sine_table,
            second_half * cosine_table - first_half * sine_table,
        ],
        axis=-1,
    )


def contract_rows(left, right):
    return lax.dot_general(
        left, right, (((0,), (0,)), ((), ())), preferred_element_type=jnp.float32
    )


def contract_cols(left, right):
    return lax.dot_general(
        left, right, (((1,), (1,)), ((), ())), preferred_element_type=jnp.float32
    )


def ring_pos(chip, chips):
    return jnp.where(chip % 2 == 0, chip // 2, chips - 1 - chip // 2)


def ring_chip(pos, chips):
    pos = pos % chips
    return jnp.where(pos < chips // 2, 2 * pos, 2 * (chips - 1 - pos) + 1)


def ring_perms(chips):
    order = list(range(0, chips, 2)) + list(range(1, chips, 2))[::-1]
    right = []
    for place in range(chips):
        for core in range(2):
            right.append((order[place] * 2 + core, order[(place + 1) % chips] * 2 + core))
    return right, [(b, a) for a, b in right], [(i, i ^ 1) for i in range(2 * chips)]


def hops(chips, flip):
    longer = chips // 2
    return (chips - 1 - longer, longer) if flip else (longer, chips - 1 - longer)


def tie(*values):
    return lax.optimization_barrier(values)


def ring_gather(block, flip):
    chips = lax.axis_size("dp") // 2
    right, left, sibling = ring_perms(chips)
    index = lax.axis_index("dp")
    core = index % 2
    place = ring_pos(index // 2, chips)
    count_right, count_left = hops(chips, flip)
    steps = max(count_right, count_left)
    whole = jnp.zeros((chips, 2) + block.shape, block.dtype)

    def put(whole, value, pos, side):
        return lax.dynamic_update_slice(
            whole, value[None, None], (ring_chip(pos, chips), side, 0, 0)
        )

    whole = put(whole, block, place, core)
    held, places = [block], [place]
    from_left, from_right = block, block
    for step in range(1, steps + 1):
        arrived = []
        if step <= count_right:
            from_left = lax.ppermute(from_left, "dp", right)
            arrived.append((from_left, place - step))
        if step <= count_left:
            from_right = lax.ppermute(from_right, "dp", left)
            arrived.append((from_right, place + step))
        proceed = yield [value for value, _ in arrived]
        if proceed is not None:
            arrived = [(value, pos) for value, (_, pos) in zip(proceed, arrived)]
            if step <= count_right:
                from_left = proceed[0]
            if step <= count_left:
                from_right = proceed[-1]
        for value, pos in arrived:
            whole = put(whole, value, pos, core)
            held.append(value)
            places.append(pos)
        if step == (steps + 1) // 2 or step == steps:
            other = lax.ppermute(jnp.stack(held), "dp", sibling)
            for number, pos in enumerate(places):
                whole = put(whole, other[number], pos, 1 - core)
            held, places = [], []
    return whole.reshape(2 * chips * block.shape[0], block.shape[1])


def ring_scatter(arrays, flip):
    chips = lax.axis_size("dp") // 2
    right, left, sibling = ring_perms(chips)
    index = lax.axis_index("dp")
    core = index % 2
    place = ring_pos(index // 2, chips)
    count_right, count_left = hops(chips, flip)
    pairs = [v.reshape(chips, 2, v.shape[0] // (2 * chips), v.shape[1]) for v in arrays]
    theirs = jnp.concatenate(
        [lax.dynamic_index_in_dim(v, 1 - core, 1, keepdims=False) for v in pairs], axis=2
    )
    got = lax.ppermute(theirs, "dp", sibling)

    def chunk(pos):
        chip = ring_chip(pos, chips)
        own = jnp.concatenate(
            [
                lax.dynamic_slice(v, (chip, core, 0, 0), (1, 1) + v.shape[2:])[0, 0]
                for v in pairs
            ],
            axis=1,
        )
        return own.astype(jnp.float32) + lax.dynamic_index_in_dim(
            got, chip, 0, keepdims=False
        ).astype(jnp.float32)

    from_left, from_right = None, None
    for step in range(max(count_right, count_left), 0, -1):
        sends = []
        if step <= count_right:
            part = chunk(place + step)
            if from_left is not None:
                part = part + from_left.astype(jnp.float32)
            sends.append(part.astype(jnp.bfloat16))
        if step <= count_left:
            part = chunk(place - step)
            if from_right is not None:
                part = part + from_right.astype(jnp.float32)
            sends.append(part.astype(jnp.bfloat16))
        proceed = yield sends
        if proceed is not None:
            sends = proceed
        if step <= count_right:
            from_left = lax.ppermute(sends[0], "dp", right)
        if step <= count_left:
            from_right = lax.ppermute(sends[-1], "dp", left)
    total = chunk(place)
    for part in (from_left, from_right):
        if part is not None:
            total = total + part.astype(jnp.float32)
    return total


class Steps:
    def __init__(self, ring):
        self.ring = ring
        self.waiting = next(ring)
        self.result = None

    def advance(self, value):
        if self.waiting is None:
            return value
        value, *values = tie(value, *self.waiting)
        try:
            self.waiting = self.ring.send(values)
        except StopIteration as end:
            self.waiting, self.result = None, end.value
        return value

    def finish(self):
        while self.waiting is not None:
            try:
                self.waiting = self.ring.send(None)
            except StopIteration as end:
                self.waiting, self.result = None, end.value
        return self.result


def shifted(values, shift):
    size = lax.axis_size("tensor")
    return lax.ppermute(values, "tensor", [((i + shift) % size, i) for i in range(size)])


def gather_parts(own):
    return [own] + [shifted(own, k) for k in range(1, lax.axis_size("tensor"))]


def scatter_parts(make_part):
    size = lax.axis_size("tensor")
    arrived = [shifted(make_part(k).astype(jnp.bfloat16), -k) for k in range(1, size)]
    total = make_part(0)
    for part in arrived:
        total = total + part.astype(jnp.float32)
    return total


def to_slots(parts):
    size = len(parts)
    rows = parts[0].shape[0]
    start = ((size - lax.axis_index("tensor")) % size) * rows
    return lax.dynamic_slice_in_dim(jnp.concatenate(parts + parts[:-1], axis=0), start, size * rows, 0)


def part_of(values, k):
    size = lax.axis_size("tensor")
    rows = values.shape[0] // size
    return lax.dynamic_slice_in_dim(
        values, ((lax.axis_index("tensor") + k) % size) * rows, rows, 0
    )


def sum_everywhere(values):
    for name in ("tensor", "dp"):
        size = lax.axis_size(name)
        bit = 1
        while bit < size:
            values = values + lax.ppermute(values, name, [(i, i ^ bit) for i in range(size)])
            bit *= 2
    return values


def per_device(
    tokens,
    lengths,
    attn_gain,
    w_query,
    key_weight,
    value_weight,
    query_gain,
    key_gain,
    w_out,
    ffn_gain,
    w_gate,
    w_up,
    w_down,
    out_grad,
):
    tok_rows = tokens.shape[0]
    group_rows = tok_rows * lax.axis_size("tensor")
    head_dim = query_gain.shape[0]
    kv_heads = key_weight.shape[1] // head_dim
    query_heads = w_query.shape[1] // head_dim
    repeat = query_heads // kv_heads
    blk_rows = min(512, group_rows)
    score_scale = head_dim ** (-0.5)
    segment_index, position, valid_mask = segments(lengths[0], group_rows)
    first_row = lax.axis_index("tensor") * tok_rows
    valid_local = lax.dynamic_slice_in_dim(valid_mask, first_row, tok_rows, 0)
    cosine_table, sine_table = rope_tables(position, head_dim)
    qgain_wide = query_gain.astype(jnp.float32)
    kgain_wide = key_gain.astype(jnp.float32)
    shard_rows = w_query.shape[0]
    qw, kw = w_query.shape[1], key_weight.shape[1]
    token_parts = gather_parts(tokens)
    grad_out = jnp.where(valid_local[:, None], out_grad, jnp.zeros_like(out_grad))
    gain_columns = jnp.concatenate(
        [
            attn_gain[:, None],
            ffn_gain[:, None],
            jnp.zeros((shard_rows, 126), jnp.bfloat16),
        ],
        axis=1,
    )
    attn_pack = Steps(
        ring_gather(
            jnp.concatenate([w_query, key_weight, value_weight, w_out.T, gain_columns], axis=1),
            False,
        )
    ).finish()
    ffn_block = jnp.concatenate([w_gate, w_up, w_down.T], axis=1)
    attn_pack, ffn_block = tie(attn_pack, ffn_block)
    ffn_ring = Steps(ring_gather(ffn_block, True))
    fw = w_gate.shape[1]
    wq_all = attn_pack[:, :qw]
    wk_all = attn_pack[:, qw : qw + kw]
    wv_all = attn_pack[:, qw + kw : qw + 2 * kw]
    wot_all = attn_pack[:, qw + 2 * kw : 2 * qw + 2 * kw]
    attn_gain_all = attn_pack[:, 2 * qw + 2 * kw]
    ffn_gain_all = attn_pack[:, 2 * qw + 2 * kw + 1]
    grad_parts = gather_parts(grad_out)
    tokens_wide = tokens.astype(jnp.float32)
    attn_inv = lax.rsqrt(jnp.mean(tokens_wide * tokens_wide, axis=-1, keepdims=True) + EPSILON)
    attn_rows = rows_normalize(
        to_slots(token_parts).astype(jnp.float32), attn_gain_all.astype(jnp.float32)
    )[0].astype(jnp.bfloat16)
    query_raw = jnp.dot(attn_rows, wq_all, preferred_element_type=jnp.float32).reshape(
        group_rows, query_heads, head_dim
    )
    key_unrotated = jnp.dot(attn_rows, wk_all, preferred_element_type=jnp.float32).reshape(
        group_rows, kv_heads, head_dim
    )
    value_lowered = (
        jnp.dot(attn_rows, wv_all, preferred_element_type=jnp.float32)
        .astype(jnp.bfloat16)
        .reshape(group_rows, kv_heads, head_dim)
    )
    query_normed, query_inv = rows_normalize(query_raw, qgain_wide)
    key_normed, key_inv = rows_normalize(key_unrotated, kgain_wide)
    query_low = apply_rotary(query_normed, cosine_table, sine_table).astype(jnp.bfloat16)
    key_low = apply_rotary(key_normed, cosine_table, sine_table).astype(jnp.bfloat16)
    query_low = ffn_ring.advance(query_low)
    query_grouped = query_low.reshape(group_rows, kv_heads, repeat, head_dim)
    outputs = []
    kept_stats = []
    for number in range(group_rows // blk_rows):
        low_row = number * blk_rows
        high_row = low_row + blk_rows
        allowed = block_mask(segment_index, valid_mask, low_row, high_row, high_row)
        scores = (
            jnp.einsum(
                "qgrd,kgd->grqk",
                query_grouped[low_row:high_row],
                key_low[:high_row],
                preferred_element_type=jnp.float32,
            )
            * score_scale
        )
        scores = jnp.where(allowed[None, None], scores, MASK_FILL)
        row_peak = jnp.max(scores, axis=-1, keepdims=True)
        exp_terms = jnp.exp(scores - row_peak)
        row_total = jnp.sum(exp_terms, axis=-1, keepdims=True)
        probs_low = (exp_terms / row_total).astype(jnp.bfloat16)
        outputs.append(
            jnp.einsum(
                "grqk,kgd->qgrd",
                probs_low,
                value_lowered[:high_row],
                preferred_element_type=jnp.float32,
            )
        )
        kept_stats.append((row_peak, row_total))
        outputs[-1] = ffn_ring.advance(outputs[-1])
        query_grouped, outputs[-1] = tie(query_grouped, outputs[-1])
    heads_low = (
        jnp.concatenate(outputs, axis=0)
        .reshape(group_rows, query_heads * head_dim)
        .astype(jnp.bfloat16)
    )
    mixed = tokens_wide + scatter_parts(lambda k: contract_cols(part_of(heads_low, k), wot_all))
    ffn_in, ffn_inv = rows_normalize(mixed, ffn_gain_all.astype(jnp.float32))
    ffn_pack = ffn_ring.finish()
    wg_all, wu_all, wdt_all = ffn_pack[:, :fw], ffn_pack[:, fw : 2 * fw], ffn_pack[:, 2 * fw :]
    ffn_parts = gather_parts(ffn_in.astype(jnp.bfloat16))
    gates, ups, hiddens, grad_gates, grad_ups = [], [], [], [], []
    for ffn_rows, grad_rows in zip(ffn_parts, grad_parts):
        gate = jnp.dot(ffn_rows, wg_all, preferred_element_type=jnp.float32)
        up_proj = jnp.dot(ffn_rows, wu_all, preferred_element_type=jnp.float32)
        grad_hidden = jnp.dot(grad_rows, wdt_all, preferred_element_type=jnp.float32)
        sigmoid_gate = jax.nn.sigmoid(gate)
        hiddens.append((gate * sigmoid_gate * up_proj).astype(jnp.bfloat16))
        grad_ups.append((grad_hidden * gate * sigmoid_gate).astype(jnp.bfloat16))
        grad_gates.append(
            (
                grad_hidden * up_proj * sigmoid_gate * (1.0 + gate * (1.0 - sigmoid_gate))
            ).astype(jnp.bfloat16)
        )
    ffn_cat = jnp.concatenate(ffn_parts, axis=0)
    grad_cat = jnp.concatenate(grad_parts, axis=0)

    def ffn_in_part(k):
        return contract_cols(grad_gates[k], wg_all) + contract_cols(grad_ups[k], wu_all)

    sends = [ffn_in_part(k).astype(jnp.bfloat16) for k in range(1, len(ffn_parts))]
    ffn_cat, *sends = tie(ffn_cat, *sends)
    grad_ffn_in = ffn_in_part(0)
    for k, part in enumerate(sends):
        grad_ffn_in = grad_ffn_in + shifted(part, -k - 1).astype(jnp.float32)
    back_mixed, ffn_gain_part = norm_back(
        mixed, ffn_inv, ffn_gain_all.astype(jnp.float32), grad_ffn_in
    )
    grad_mixed = grad_out.astype(jnp.float32) + back_mixed
    mixed_low, grad_cat = tie(grad_mixed.astype(jnp.bfloat16), grad_cat)
    mixed_parts = gather_parts(mixed_low)
    mixed_parts[-1], *late = tie(mixed_parts[-1], *hiddens)
    result = mixed + scatter_parts(lambda k: contract_cols(late[k], wdt_all))
    output = result.astype(jnp.bfloat16)
    ffn_sum_ring = Steps(
        ring_scatter(
            [
                contract_rows(ffn_cat, jnp.concatenate(grad_gates, axis=0)).astype(jnp.bfloat16),
                contract_rows(ffn_cat, jnp.concatenate(grad_ups, axis=0)).astype(jnp.bfloat16),
                contract_rows(grad_cat, jnp.concatenate(hiddens, axis=0)).astype(jnp.bfloat16),
            ],
            False,
        )
    )
    grad_heads = to_slots(
        [
            jnp.dot(rows, wot_all, preferred_element_type=jnp.float32).astype(jnp.bfloat16)
            for rows in mixed_parts
        ]
    ).reshape(group_rows, kv_heads, repeat, head_dim)
    grad_wot = contract_rows(to_slots(mixed_parts), heads_low)
    grad_query_parts = []
    grad_key = jnp.zeros((group_rows, kv_heads, head_dim), jnp.float32)
    grad_value = jnp.zeros((group_rows, kv_heads, head_dim), jnp.float32)
    for number in range(group_rows // blk_rows):
        low_row = number * blk_rows
        high_row = low_row + blk_rows
        row_peak, row_total = kept_stats[number]
        row_peak = ffn_sum_ring.advance(row_peak)
        allowed = block_mask(segment_index, valid_mask, low_row, high_row, high_row)
        scores = (
            jnp.einsum(
                "qgrd,kgd->grqk",
                query_grouped[low_row:high_row],
                key_low[:high_row],
                preferred_element_type=jnp.float32,
            )
            * score_scale
        )
        scores = jnp.where(allowed[None, None], scores, MASK_FILL)
        probs_wide = jnp.exp(scores - row_peak) / row_total
        probs_low = probs_wide.astype(jnp.bfloat16)
        grad_probs = jnp.einsum(
            "qgrd,kgd->grqk",
            grad_heads[low_row:high_row],
            value_lowered[:high_row],
            preferred_element_type=jnp.float32,
        )
        inner_sum = jnp.sum(probs_wide * grad_probs, axis=-1, keepdims=True)
        grad_scores = (probs_wide * (grad_probs - inner_sum)).astype(jnp.bfloat16)
        grad_scores = ffn_sum_ring.advance(grad_scores)
        grad_query_parts.append(
            jnp.einsum(
                "grqk,kgd->qgrd",
                grad_scores,
                key_low[:high_row],
                preferred_element_type=jnp.float32,
            )
            * score_scale
        )
        grad_key = grad_key.at[:high_row].add(
            jnp.einsum(
                "grqk,qgrd->kgd",
                grad_scores,
                query_grouped[low_row:high_row],
                preferred_element_type=jnp.float32,
            )
            * score_scale
        )
        grad_value = grad_value.at[:high_row].add(
            jnp.einsum(
                "grqk,qgrd->kgd",
                probs_low,
                grad_heads[low_row:high_row],
                preferred_element_type=jnp.float32,
            )
        )
    grad_query_all = jnp.concatenate(grad_query_parts, axis=0).reshape(
        group_rows, query_heads, head_dim
    )
    grad_query_raw, qgain_terms = norm_back(
        query_raw, query_inv, qgain_wide, unrotate(grad_query_all, cosine_table, sine_table)
    )
    grad_key_raw, kgain_terms = norm_back(
        key_unrotated, key_inv, kgain_wide, unrotate(grad_key, cosine_table, sine_table)
    )
    grad_query_low = grad_query_raw.reshape(group_rows, query_heads * head_dim).astype(jnp.bfloat16)
    grad_key_low = grad_key_raw.reshape(group_rows, kv_heads * head_dim).astype(jnp.bfloat16)
    grad_value_low = grad_value.reshape(group_rows, kv_heads * head_dim).astype(jnp.bfloat16)
    grad_wq = contract_rows(attn_rows, grad_query_low)
    grad_wk = contract_rows(attn_rows, grad_key_low)
    grad_wv = contract_rows(attn_rows, grad_value_low)
    attn_in_parts = [
        contract_cols(part_of(grad_query_low, k), wq_all)
        + contract_cols(part_of(grad_key_low, k), wk_all)
        + contract_cols(part_of(grad_value_low, k), wv_all)
        for k in range(len(token_parts))
    ]
    grad_attn_in = scatter_parts(lambda k: attn_in_parts[k])
    back_tokens, _ = norm_back(
        tokens_wide, attn_inv, attn_gain_all.astype(jnp.float32), grad_attn_in
    )
    attn_gain_sum = 0.0
    for part, rows in zip(attn_in_parts, token_parts):
        normed = rows_normalize(rows.astype(jnp.float32), 1.0)[0]
        attn_gain_sum = attn_gain_sum + jnp.sum(part * normed, axis=0)
    input_grad = grad_mixed + back_tokens
    ffn_sum = ffn_sum_ring.finish()
    ffn_sums = (ffn_sum[:, :fw], ffn_sum[:, fw : 2 * fw], ffn_sum[:, 2 * fw :].T)
    attn_pack_sum = Steps(
        ring_scatter(
            [v.astype(jnp.bfloat16) for v in (grad_wq, grad_wk, grad_wv, grad_wot)], True
        )
    ).finish()
    attn_sums = (
        attn_pack_sum[:, :qw],
        attn_pack_sum[:, qw : qw + kw],
        attn_pack_sum[:, qw + kw : qw + 2 * kw],
        attn_pack_sum[:, qw + 2 * kw :].T,
    )
    width = tokens.shape[1]
    summed = sum_everywhere(
        jnp.concatenate(
            [
                attn_gain_sum,
                jnp.sum(ffn_gain_part, axis=0),
                jnp.sum(qgain_terms, axis=(0, 1)),
                jnp.sum(kgain_terms, axis=(0, 1)),
            ]
        )
    )
    gain_sums = (
        summed[:width],
        summed[width : 2 * width],
        summed[2 * width : 2 * width + head_dim],
        summed[2 * width + head_dim :],
    )
    gain_shard = attn_gain.shape[0]
    gain_start = lax.axis_index("dp") * gain_shard
    attn_gain_grad = lax.dynamic_slice_in_dim(gain_sums[0], gain_start, gain_shard, 0)
    ffn_gain_grad = lax.dynamic_slice_in_dim(gain_sums[1], gain_start, gain_shard, 0)
    return (
        output,
        input_grad,
        attn_gain_grad,
        attn_sums[0],
        attn_sums[1],
        attn_sums[2],
        gain_sums[2],
        gain_sums[3],
        attn_sums[3],
        ffn_gain_grad,
        ffn_sums[0],
        ffn_sums[1],
        ffn_sums[2],
    )


def solution(mesh):
    in_specs = (
        P(("dp", "tensor"), None),
        P("dp", None),
        P("dp"),
        P("dp", "tensor"),
        P("dp", "tensor"),
        P("dp", "tensor"),
        P(),
        P(),
        P("tensor", "dp"),
        P("dp"),
        P("dp", "tensor"),
        P("dp", "tensor"),
        P("tensor", "dp"),
        P(("dp", "tensor"), None),
    )
    out_specs = (
        P(("dp", "tensor"), None),
        P(("dp", "tensor"), None),
        P("dp"),
        P("dp", "tensor"),
        P("dp", "tensor"),
        P("dp", "tensor"),
        P(),
        P(),
        P("tensor", "dp"),
        P("dp"),
        P("dp", "tensor"),
        P("dp", "tensor"),
        P("tensor", "dp"),
    )
    return jax.shard_map(
        per_device, mesh=mesh, in_specs=in_specs, out_specs=out_specs, check_vma=False
    )
```
